32 devices in a mesh: branch: 8 (over y, x, core), head: 4 (over z).
Axes of the slice: x: 2, y: 2, z: 4, core: 2. Of those that a mesh axis runs over, the one named last changes fastest.
Arguments:
- queries: bfloat16 [4, 8, 256, 8192], P(None, 'branch', None, 'head'), may hold values from -96 to 96
- key_rows: bfloat16 [4, 8, 256, 1024], P(None, 'branch', None, 'head'), may hold values from -4 to 4
- value_rows: bfloat16 [4, 8, 256, 1024], P(None, 'branch', None, 'head'), may hold values from -5 to 5
- cotangent: bfloat16 [4, 8, 256, 8192], P(None, 'branch', None, 'head'), may hold values from -6 to 6
- out_weight: bfloat16 [8192, 8192], P('head'), may hold values from -0.0625 to 0.0625
- parents: int32 [3, 8], replicated, may hold values from 0 to 7
- seg_len: int32 [4, 8], replicated, may hold values from 128 to 256, as said below
Outputs:
- query_grad: bfloat16 [4, 8, 256, 8192], P(None, 'branch', None, 'head')
- key_grad: bfloat16 [4, 8, 256, 1024], P(None, 'branch', None, 'head')
- value_grad: bfloat16 [4, 8, 256, 1024], P(None, 'branch', None, 'head')
The draws below stay inside these ranges and needn't reach their ends.
Inputs may be any that keep to these rules, and one draw needn't show every extreme that they name: parents[m, j] is the node of level m that node j of level m + 1 continues; a node may have many children or none. `seg_len`: some node uses all 256 slots in every draw.
All inputs are finite; a program needn't handle non-finite values.
Results may differ from the reference program's by a relative error of at most 0.015.
Values may be sent and summed in bfloat16 or wider, within the bound.
A program may use at most 192 MiB of HBM per device.

```python
import math
import jax
import jax.numpy as jnp
import numpy as np
from jax import lax

D = 8192
HEADS = 64
KVH = 8
HD = 128
LEVELS = 4
SEG = 256
NODES = 8


def shared_keys(key):
    sample_rows = jax.random.normal(key, (LEVELS, NODES, SEG, KVH * HD), jnp.float32)
    return jnp.clip(sample_rows, -4.0, 4.0)


def draw_key_rows(key, part):
    baseline = shared_keys(key)
    return baseline.astype(jnp.bfloat16)


def draw_queries(key, part):
    key = jax.random.fold_in(key, 5)
    sample_rows = jnp.clip(jax.random.normal(key, (LEVELS, NODES, SEG, HEADS * HD), jnp.float32), -4.0, 4.0)
    return sample_rows.astype(jnp.bfloat16)


def draw_seg_len(key, part):
    key = jax.random.fold_in(key, 9)
    first_key, second_key = jax.random.split(key)
    lengths = jax.random.randint(first_key, (LEVELS, NODES), SEG // 2, SEG + 1, jnp.int32)
    chosen = jax.random.randint(second_key, (), 0, LEVELS * NODES, jnp.int32)
    flattened = lengths.reshape(-1).at[chosen].set(SEG)
    return flattened.reshape(LEVELS, NODES).astype(jnp.int32)


def place_ends(array, stream_key, low, top_value):
    shape = array.shape
    place = [jax.random.randint(jax.random.fold_in(stream_key, axis), (), 0, shape[axis]) for axis in range(len(shape))]
    array = array.at[tuple(place)].set(low)
    longest = shape.index(max(shape))
    place[longest] = (place[longest] + 1) % shape[longest]
    return array.at[tuple(place)].set(top_value)


def level_of(own_key, dims, shards, low, high):
    level = 1.0
    for dim, blocks in shards:
        steps = jax.random.uniform(jax.random.fold_in(jax.random.fold_in(own_key, 6), dim), (blocks,), jnp.float32, low / len(shards), high / len(shards))
        level = level * jnp.repeat(jnp.exp(steps), dims[dim] // blocks).reshape((-1,) + (1,) * (len(dims) - 1 - dim))
    return level


def cumulative_ranks(amount, slope):
    weights = [(1 << 20) // math.isqrt(grade ** slope) + 1 for grade in range(1, amount + 1)]
    scale = 1 + sum(weights) // (1 << 30)
    return np.cumsum(np.array([max(1, weight // scale) for weight in weights]))


def skewed_ids(rng, dims, count, lean):
    table = cumulative_ranks(count, lean)
    pick = jax.random.randint(jax.random.fold_in(rng, 1), dims, 0, int(table[count - 1]))
    rank = jnp.searchsorted(jnp.asarray(table, jnp.int32), pick, side="right")
    return jax.random.permutation(jax.random.fold_in(rng, 2), count)[rank].astype(jnp.int32)


def normal_values(rng, shape, spread, reach, pieces=(), kind=jnp.bfloat16):
    loudness = level_of(rng, shape, pieces, -0.22, 0.18) if pieces else 1.0
    entries = jax.random.normal(rng, shape, jnp.float32) * spread * loudness
    return jnp.minimum(jnp.maximum(entries, -reach), reach).astype(kind)


def setup_inputs(seed: int = 0) -> dict:
    seeds = jax.random.split(jax.random.key(seed), 8)
    return {
        "queries": draw_queries(jax.random.fold_in(seeds[7], 71), 0),
        "key_rows": draw_key_rows(jax.random.fold_in(seeds[7], 71), 0),
        "value_rows": normal_values(seeds[2], (LEVELS, NODES, SEG, KVH * HD), 1.0, 5.0, ((1, 8), (3, 4))),
        "cotangent": normal_values(seeds[3], (LEVELS, NODES, SEG, D), 1.0, 6.0, ((1, 8), (3, 4))),
        "out_weight": normal_values(seeds[4], (HEADS * HD, D), D ** -0.5, 0.0625, ((0, 4),)),
        "parents": place_ends(skewed_ids(seeds[5], (LEVELS - 1, NODES), NODES, 2), jax.random.fold_in(seeds[5], 3), 0, NODES - 1).astype(jnp.int32),
        "seg_len": draw_seg_len(jax.random.fold_in(seeds[7], 71), 0),
    }


masked_score = -1e30


def lineage_of(parents, level_index):
    node_count = parents.shape[1]
    lineage = [None] * (level_index + 1)
    lineage[level_index] = jnp.arange(node_count, dtype=jnp.int32)
    for ancestor_level in reversed(range(level_index)):
        lineage[ancestor_level] = parents[ancestor_level][lineage[ancestor_level + 1]].astype(jnp.int32)
    return lineage


def rounded(array_in):
    narrow = lax.optimization_barrier(array_in.astype(jnp.bfloat16))
    return narrow.astype(jnp.float32)


def reference(queries, key_rows, value_rows, cotangent, out_weight, parents, seg_len):
    levels, node_count, seg_rows, q_width = queries.shape
    group_size = HEADS // KVH
    logit_scale = 1.0 / (HD ** 0.5)
    dout = jnp.dot(cotangent.reshape(-1, D), out_weight.T, preferred_element_type=jnp.float32)
    dout = dout.astype(jnp.bfloat16).reshape(levels, node_count, seg_rows, KVH, group_size, HD)
    positions = jnp.arange(seg_rows)
    query_mask = positions[None, None, :] < seg_len[:, :, None]
    dout = jnp.where(query_mask[:, :, :, None, None, None], dout, jnp.zeros_like(dout))
    query_split = queries.reshape(levels, node_count, seg_rows, KVH, group_size, HD)
    key_split = key_rows.reshape(levels, node_count, seg_rows, KVH, HD)
    value_split = value_rows.reshape(levels, node_count, seg_rows, KVH, HD)
    key_total = jnp.zeros((levels, node_count, seg_rows, KVH, HD), jnp.float32)
    value_total = jnp.zeros((levels, node_count, seg_rows, KVH, HD), jnp.float32)
    query_levels = []
    for level_index in range(levels):
        lineage = lineage_of(parents, level_index)
        key_cat = jnp.concatenate([key_split[m][lineage[m]] for m in range(level_index + 1)], axis=1)
        value_cat = jnp.concatenate([value_split[m][lineage[m]] for m in range(level_index + 1)], axis=1)
        allowed_blocks = []
        for ancestor_level in range(level_index):
            length = seg_len[ancestor_level][lineage[ancestor_level]]
            allowed_blocks.append(jnp.broadcast_to((positions[None, None, :] < length[:, None, None]), (node_count, seg_rows, seg_rows)))
        own_length = seg_len[level_index]
        own_allowed = (positions[None, None, :] <= positions[None, :, None]) & (positions[None, None, :] < own_length[:, None, None])
        allowed_blocks.append(own_allowed)
        allowed = jnp.concatenate(allowed_blocks, axis=2)

        def one_head(operands):
            query_head, key_head, value_head, dout_head = operands
            query_wide = query_head.astype(jnp.float32)
            key_wide = key_head.astype(jnp.float32)
            value_wide = value_head.astype(jnp.float32)
            output_gradient_wide = dout_head.astype(jnp.float32)
            score_matrix = jnp.einsum('surf,stf->srut', query_wide, key_wide) * logit_scale
            score_matrix = jnp.where(allowed[:, None], score_matrix, masked_score)
            maximum = jnp.max(score_matrix, axis=-1, keepdims=True)
            exponent = jnp.exp(score_matrix - maximum)
            softmax = exponent / jnp.sum(exponent, axis=-1, keepdims=True)
            probability_narrow = rounded(softmax)
            attention_weights = jnp.einsum('noha,naf->nhof', probability_narrow, value_wide)
            delta_rows = jnp.sum(output_gradient_wide * attention_weights, axis=-1)
            probability_gradient = jnp.einsum('surf,stf->srut', output_gradient_wide, value_wide)
            dscores = softmax * (probability_gradient - jnp.transpose(delta_rows, (0, 2, 1))[..., None])
            score_gradient_narrow = rounded(dscores)
            query_portion = jnp.einsum('noha,naf->nhof', score_gradient_narrow, key_wide) * logit_scale
            key_portion = jnp.einsum('fiuh,fuip->fhp', score_gradient_narrow, query_wide) * logit_scale
            value_portion = jnp.einsum('fiuh,fuip->fhp', probability_narrow, output_gradient_wide)
            return query_portion, key_portion, value_portion

        operands = (jnp.moveaxis(query_split[level_index], 2, 0), jnp.moveaxis(key_cat, 2, 0),
                    jnp.moveaxis(value_cat, 2, 0), jnp.moveaxis(dout[level_index], 2, 0))
        query_portion, key_portion, value_portion = lax.map(one_head, operands)
        query_levels.append(jnp.moveaxis(query_portion, 0, 2).astype(jnp.bfloat16).reshape(node_count, seg_rows, q_width))
        key_portion = jnp.moveaxis(key_portion, 0, 2)
        value_portion = jnp.moveaxis(value_portion, 0, 2)
        for ancestor_level in range(level_index + 1):
            start = ancestor_level * seg_rows
            key_total = key_total.at[ancestor_level, lineage[ancestor_level]].add(key_portion[:, start:start + seg_rows])
            value_total = value_total.at[ancestor_level, lineage[ancestor_level]].add(value_portion[:, start:start + seg_rows])
    query_grad = jnp.stack(query_levels, axis=0)
    key_grad = key_total.astype(jnp.bfloat16).reshape(levels, node_count, seg_rows, KVH * HD)
    value_grad = value_total.astype(jnp.bfloat16).reshape(levels, node_count, seg_rows, KVH * HD)
    return (query_grad, key_grad, value_grad)
```

```python
import functools

import jax
import jax.numpy as jnp
from jax import lax
from jax.experimental import pallas as pl
from jax.experimental.pallas import tpu as pltpu
from jax.sharding import PartitionSpec as P

HD = 128
MASKED = -1e30
NT = (((1,), (1,)), ((), ()))
NN = (((1,), (0,)), ((), ()))
TN = (((0,), (0,)), ((), ()))


def pick_row(table, index_value):
    return lax.dynamic_index_in_dim(table, index_value, 0, keepdims=False)


def attention_kernel(level, has_base, info_ref, q_ref, dout_ref, *refs):
    blocks = level + 1
    key_refs, value_refs = refs[:blocks], refs[blocks : 2 * blocks]
    dq_ref, dk_ref, dv_ref = refs[2 * blocks + has_base :]
    seg = dout_ref.shape[0]
    scale = 1.0 / HD**0.5
    q = q_ref[...].reshape(seg, HD)
    own_len = info_ref[4 + level]
    dout = dout_ref[...]
    row = lax.broadcasted_iota(jnp.int32, (seg, HD), 0)
    dout = jnp.where(row < own_len, dout, jnp.zeros_like(dout))
    keys = [ref[...].reshape(seg, HD) for ref in key_refs]
    values = [ref[...].reshape(seg, HD) for ref in value_refs]
    key_pos = lax.broadcasted_iota(jnp.int32, (seg, seg), 0)
    query_pos = lax.broadcasted_iota(jnp.int32, (seg, seg), 1)

    def dot(a, b, dims):
        return lax.dot_general(a, b, dims, preferred_element_type=jnp.float32)

    scores = []
    for m in range(blocks):
        allowed = key_pos < info_ref[4 + m]
        if m == level:
            allowed = allowed & (key_pos <= query_pos)
        scores.append(jnp.where(allowed, dot(keys[m], q, NT) * scale, MASKED))
    top = functools.reduce(jnp.maximum, [jnp.max(s, axis=0, keepdims=True) for s in scores])
    exps = [jnp.exp(s - top) for s in scores]
    total = functools.reduce(jnp.add, [jnp.sum(e, axis=0, keepdims=True) for e in exps])
    inverse = 1.0 / total
    probs = [e * inverse for e in exps]
    narrow = [p.astype(jnp.bfloat16) for p in probs]
    dprobs = [dot(v, dout, NT) for v in values]
    delta = functools.reduce(
        jnp.add,
        [
            jnp.sum(pb.astype(jnp.float32) * dp, axis=0, keepdims=True)
            for pb, dp in zip(narrow, dprobs)
        ],
    )

    @pl.when(pl.program_id(1) == 0)
    def _():
        dk_ref[...] = jnp.zeros_like(dk_ref)
        dv_ref[...] = jnp.zeros_like(dv_ref)

    dq = jnp.zeros((HD, seg), jnp.float32)
    for m in range(blocks):
        ds = (probs[m] * (dprobs[m] - delta)).astype(jnp.bfloat16)
        dk_ref[m] += dot(ds, q, NN) * scale
        dv_ref[m] += dot(narrow[m], dout, NN)
        dq = dq + dot(keys[m], ds, TN)
    dq_ref[...] = (dq * scale).T.astype(jnp.bfloat16).reshape(dq_ref.shape)


def attention_level(level, info, queries, dout, key_rows, value_rows, kv_all, base):
    levels, _, seg, q_width = queries.shape
    kv_width = key_rows.shape[3]
    kv_local = kv_width // HD
    group = q_width // kv_width
    blocks = level + 1

    def gathered(kind, m):
        return pl.BlockSpec(
            (1, 1, 1, seg, HD), lambda n, g, info, m=m, k=kind: (info[m], m, k, 0, n)
        )

    q_spec = pl.BlockSpec((1, 1, seg, HD), lambda n, g, info: (level, 0, 0, n * group + g))
    own_spec = pl.BlockSpec((1, 1, seg, HD), lambda n, g, info: (level, 0, 0, n))
    head_spec = pl.BlockSpec((seg, HD), lambda n, g, info: (0, n * group + g))
    grad_spec = pl.BlockSpec((blocks, seg, HD), lambda n, g, info: (0, 0, n))
    in_specs = [q_spec, head_spec]
    in_specs += [gathered(0, m) for m in range(level)] + [own_spec]
    in_specs += [gathered(1, m) for m in range(level)] + [own_spec]
    operands = [queries, dout] + [kv_all] * level + [key_rows] + [kv_all] * level + [value_rows]
    aliases = {}
    if base is not None:
        in_specs.append(pl.BlockSpec(memory_space=pl.ANY))
        operands.append(base)
        aliases = {len(operands): 0}
    grad_shape = jax.ShapeDtypeStruct((blocks, seg, kv_width), jnp.float32)
    products = 5 * 2 * seg * seg * HD * blocks * kv_local * group
    return pl.pallas_call(
        functools.partial(attention_kernel, level, int(base is not None)),
        grid_spec=pltpu.PrefetchScalarGridSpec(
            num_scalar_prefetch=1,
            grid=(kv_local, group),
            in_specs=in_specs,
            out_specs=[q_spec, grad_spec, grad_spec],
        ),
        out_shape=[jax.ShapeDtypeStruct(queries.shape, jnp.bfloat16), grad_shape, grad_shape],
        input_output_aliases=aliases,
        compiler_params=pltpu.CompilerParams(vmem_limit_bytes=40 * 1024 * 1024),
        cost_estimate=pl.CostEstimate(
            flops=4 * products,
            bytes_accessed=3 * seg * q_width * 2,
            transcendentals=seg * seg * blocks * kv_local * group,
        ),
        name="attention_level",
    )(info, *operands)


def local(node_count, queries, key_rows, value_rows, cotangent, out_weight, parents, seg_len):
    levels, _, seg, q_width = queries.shape
    bits = node_count.bit_length() - 1
    me = lax.axis_index("branch")

    def swap(array, bit):
        pairs = [(i, i ^ (1 << bit)) for i in range(node_count)]
        return lax.ppermute(array, "branch", pairs)

    gathered = [None] * levels
    for level in reversed(range(levels)):
        gathered[level] = lax.all_gather(cotangent[level, 0], "head", axis=1, tiled=True)

    kv_all = jnp.stack([key_rows[: levels - 1, 0], value_rows[: levels - 1, 0]], axis=1)[None]
    for bit in reversed(range(bits)):
        kv_all = jnp.concatenate([kv_all, swap(kv_all, bit)], axis=0)

    offsets = []
    infos = []
    for level in range(levels):
        lineage = [None] * (level + 1)
        lineage[level] = me
        for m in reversed(range(level)):
            lineage[m] = pick_row(parents[m], lineage[m + 1])
        relative = [node ^ me for node in lineage]
        slots = [
            sum(((r >> b) & 1) << (bits - 1 - b) for b in range(bits)) for r in relative
        ]
        lengths = [pick_row(seg_len[m], lineage[m]) for m in range(level + 1)]
        pad = [jnp.int32(0)] * (levels - 1 - level)
        infos.append(jnp.stack(slots + pad + lengths + pad).astype(jnp.int32))
        offsets.append(relative)

    key_terms = [[] for _ in range(levels)]
    key_grads = [None] * levels
    value_grads = [None] * levels
    query_grad = None
    for level in reversed(range(levels)):
        dout = lax.dot_general(
            gathered[level], out_weight, NT, preferred_element_type=jnp.float32
        ).astype(jnp.bfloat16)
        query_grad, dk, dv = attention_level(
            level, infos[level], queries, dout, key_rows, value_rows, kv_all, query_grad
        )
        own = jnp.stack([dk[level], dv[level]])
        if level < levels - 1:
            own = own + received
        key_grads[level] = own[0].astype(jnp.bfloat16)
        value_grads[level] = own[1].astype(jnp.bfloat16)
        for m in range(level):
            key_terms[m].append((offsets[level][m], dk[m], dv[m]))
        if level > 0:
            m = level - 1

            def spread(ids):
                total = jnp.zeros((len(ids), 2, seg, key_rows.shape[3]), jnp.float32)
                for offset, dk_term, dv_term in key_terms[m]:
                    hit = (jnp.array(ids, jnp.int32) == offset)[:, None, None, None]
                    total = total + jnp.where(hit, jnp.stack([dk_term, dv_term])[None], 0.0)
                return total

            keep = spread(range(0, node_count, 2))
            send = spread(range(1, node_count, 2)).astype(jnp.bfloat16)
            for bit in range(bits):
                held = keep + swap(send, bit).astype(jnp.float32)
                if bit + 1 < bits:
                    keep = held[0::2]
                    send = held[1::2].astype(jnp.bfloat16)
            received = held[0]
    key_grad = jnp.stack(key_grads)[:, None]
    value_grad = jnp.stack(value_grads)[:, None]
    return query_grad, key_grad, value_grad


def solution(mesh):
    wide = P(None, "branch", None, "head")
    in_specs = (wide, wide, wide, wide, P("head", None), P(), P())
    return jax.shard_map(
        functools.partial(local, mesh.shape["branch"]),
        mesh=mesh,
        in_specs=in_specs,
        out_specs=(wide, wide, wide),
        check_vma=False,
    )
```

```python
import functools

import jax
import jax.numpy as jnp
from jax import lax
from jax.experimental import pallas as pl
from jax.experimental.pallas import tpu as pltpu
from jax.sharding import PartitionSpec as P

HD = 128
MASKED = -1e30
NT = (((1,), (1,)), ((), ()))
NN = (((1,), (0,)), ((), ()))
TN = (((0,), (0,)), ((), ()))


def pick_row(table, index_value):
    return lax.dynamic_index_in_dim(table, index_value, 0, keepdims=False)


def attention_kernel(level, has_base, info_ref, q_ref, cot_ref, weight_ref, *refs):
    blocks = level + 1
    key_refs, value_refs = refs[:blocks], refs[blocks : 2 * blocks]
    dq_ref, dk_ref, dv_ref = refs[2 * blocks + has_base :]
    seg = cot_ref.shape[0]
    heads = weight_ref.shape[0] // HD
    scale = 1.0 / HD**0.5
    own_len = info_ref[4 + level]
    keys = [ref[...].reshape(seg, HD) for ref in key_refs]
    values = [ref[...].reshape(seg, HD) for ref in value_refs]
    key_pos = lax.broadcasted_iota(jnp.int32, (seg, seg), 0)
    query_pos = lax.broadcasted_iota(jnp.int32, (seg, seg), 1)

    def dot(a, b, dims):
        return lax.dot_general(a, b, dims, preferred_element_type=jnp.float32)

    @pl.when(pl.program_id(1) == 0)
    def _():
        dk_ref[...] = jnp.zeros_like(dk_ref)
        dv_ref[...] = jnp.zeros_like(dv_ref)

    douts = dot(cot_ref[...], weight_ref[...], NT).astype(jnp.bfloat16)
    row = lax.broadcasted_iota(jnp.int32, douts.shape, 0)
    douts = jnp.where(row < own_len, douts, jnp.zeros_like(douts))
    for h in range(heads):
        columns = slice(h * HD, (h + 1) * HD)
        q = q_ref[0, 0, :, columns]
        dout = douts[:, columns]
        scores = []
        for m in range(blocks):
            allowed = key_pos < info_ref[4 + m]
            if m == level:
                allowed = allowed & (key_pos <= query_pos)
            scores.append(jnp.where(allowed, dot(keys[m], q, NT) * scale, MASKED))
        top = functools.reduce(jnp.maximum, [jnp.max(s, axis=0, keepdims=True) for s in scores])
        exps = [jnp.exp(s - top) for s in scores]
        total = functools.reduce(jnp.add, [jnp.sum(e, axis=0, keepdims=True) for e in exps])
        inverse = 1.0 / total
        probs = [e * inverse for e in exps]
        narrow = [p.astype(jnp.bfloat16) for p in probs]
        dprobs = [dot(v, dout, NT) for v in values]
        delta = functools.reduce(
            jnp.add,
            [
                jnp.sum(pb.astype(jnp.float32) * dp, axis=0, keepdims=True)
                for pb, dp in zip(narrow, dprobs)
            ],
        )
        dq = jnp.zeros((HD, seg), jnp.float32)
        for m in range(blocks):
            ds = (probs[m] * (dprobs[m] - delta)).astype(jnp.bfloat16)
            dk_ref[m] += dot(ds, q, NN) * scale
            dv_ref[m] += dot(narrow[m], dout, NN)
            dq = dq + dot(keys[m], ds, TN)
        dq_ref[0, 0, :, columns] = (dq * scale).T.astype(jnp.bfloat16)


def attention_level(level, info, queries, cot, weight, key_rows, value_rows, kv_all, base):
    levels, _, seg, q_width = queries.shape
    kv_width = key_rows.shape[3]
    kv_local = kv_width // HD
    group = q_width // kv_width
    blocks = level + 1
    heads = 2
    steps = group // heads
    model = weight.shape[1]

    def gathered(kind, m):
        return pl.BlockSpec(
            (1, 1, 1, seg, HD), lambda n, g, info, m=m, k=kind: (info[m], m, k, 0, n)
        )

    q_spec = pl.BlockSpec(
        (1, 1, seg, heads * HD), lambda n, g, info: (level, 0, 0, n * steps + g)
    )
    own_spec = pl.BlockSpec((1, 1, seg, HD), lambda n, g, info: (level, 0, 0, n))
    cot_spec = pl.BlockSpec((seg, model), lambda n, g, info: (0, 0))
    weight_spec = pl.BlockSpec((heads * HD, model), lambda n, g, info: (n * steps + g, 0))
    grad_spec = pl.BlockSpec((blocks, seg, HD), lambda n, g, info: (0, 0, n))
    in_specs = [q_spec, cot_spec, weight_spec]
    in_specs += [gathered(0, m) for m in range(level)] + [own_spec]
    in_specs += [gathered(1, m) for m in range(level)] + [own_spec]
    operands = [queries, cot, weight]
    operands += [kv_all] * level + [key_rows] + [kv_all] * level + [value_rows]
    aliases = {}
    if base is not None:
        in_specs.append(pl.BlockSpec(memory_space=pl.ANY))
        operands.append(base)
        aliases = {len(operands): 0}
    grad_shape = jax.ShapeDtypeStruct((blocks, seg, kv_width), jnp.float32)
    products = 5 * 2 * seg * seg * HD * blocks * kv_local * group
    return pl.pallas_call(
        functools.partial(attention_kernel, level, int(base is not None)),
        grid_spec=pltpu.PrefetchScalarGridSpec(
            num_scalar_prefetch=1,
            grid=(kv_local, steps),
            in_specs=in_specs,
            out_specs=[q_spec, grad_spec, grad_spec],
        ),
        out_shape=[jax.ShapeDtypeStruct(queries.shape, jnp.bfloat16), grad_shape, grad_shape],
        input_output_aliases=aliases,
        compiler_params=pltpu.CompilerParams(vmem_limit_bytes=48 * 1024 * 1024),
        cost_estimate=pl.CostEstimate(
            flops=4 * products + 2 * seg * model * q_width,
            bytes_accessed=3 * seg * q_width * 2 + q_width * model * 2,
            transcendentals=seg * seg * blocks * kv_local * group,
        ),
        name="attention_level",
    )(info, *operands)


def local(node_count, head_count, queries, key_rows, value_rows, cotangent, out_weight, parents, seg_len):
    levels, _, seg, q_width = queries.shape
    bits = node_count.bit_length() - 1
    me = lax.axis_index("branch")

    def swap(array, bit):
        pairs = [(i, i ^ (1 << bit)) for i in range(node_count)]
        return lax.ppermute(array, "branch", pairs)

    line_level = 1
    place = lax.axis_index("head")
    width = cotangent.shape[3]
    gathered = [None] * levels
    for level in reversed(range(levels)):
        if level != line_level:
            gathered[level] = lax.all_gather(cotangent[level, 0], "head", axis=1, tiled=True)
    line = cotangent[line_level, 0]
    uphill = [line]
    downhill = [line]

    def hop():
        done = len(uphill)
        up = [(i, i + 1) for i in range(done - 1, head_count - 1)]
        down = [(i + 1, i) for i in range(head_count - done)]
        uphill.append(lax.ppermute(uphill[-1], "head", up))
        downhill.append(lax.ppermute(downhill[-1], "head", down))

    kv_all = jnp.stack([key_rows[: levels - 1, 0], value_rows[: levels - 1, 0]], axis=1)[None]
    for bit in reversed(range(bits)):
        kv_all = jnp.concatenate([kv_all, swap(kv_all, bit)], axis=0)

    offsets = []
    infos = []
    for level in range(levels):
        lineage = [None] * (level + 1)
        lineage[level] = me
        for m in reversed(range(level)):
            lineage[m] = pick_row(parents[m], lineage[m + 1])
        relative = [node ^ me for node in lineage]
        slots = [
            sum(((r >> b) & 1) << (bits - 1 - b) for b in range(bits)) for r in relative
        ]
        lengths = [pick_row(seg_len[m], lineage[m]) for m in range(level + 1)]
        pad = [jnp.int32(0)] * (levels - 1 - level)
        infos.append(jnp.stack(slots + pad + lengths + pad).astype(jnp.int32))
        offsets.append(relative)

    key_terms = [[] for _ in range(levels)]
    received = [None] * levels
    key_grads = [None] * levels
    value_grads = [None] * levels
    query_grad = None
    for level in reversed(range(levels)):
        if level == line_level:
            while len(uphill) < head_count:
                hop()
            whole = jnp.zeros((seg, head_count * width), cotangent.dtype)
            whole = lax.dynamic_update_slice(whole, line, (0, place * width))
            for j in range(1, head_count):
                ahead = place + j < head_count
                piece = jnp.where(ahead, downhill[j], uphill[head_count - j])
                at = lax.rem(place + j, head_count) * width
                whole = lax.dynamic_update_slice(whole, piece, (0, at))
            gathered[level] = whole
        elif level > line_level and len(uphill) < head_count:
            hop()
            gathered[level], uphill[-1], downhill[-1] = lax.optimization_barrier(
                (gathered[level], uphill[-1], downhill[-1])
            )
        if level <= line_level:
            due = range(level + 1 if level else 0, levels - 1)
            for m in due:
                gathered[level], received[m] = lax.optimization_barrier(
                    (gathered[level], received[m])
                )
        query_grad, dk, dv = attention_level(
            level, infos[level], queries, gathered[level], out_weight,
            key_rows, value_rows, kv_all, query_grad,
        )
        own = jnp.stack([dk[level], dv[level]])
        if level < levels - 1:
            own = own + received[level]
        key_grads[level] = own[0].astype(jnp.bfloat16)
        value_grads[level] = own[1].astype(jnp.bfloat16)
        for m in range(level):
            key_terms[m].append((offsets[level][m], dk[m], dv[m]))
        if level > 0:
            m = level - 1

            def spread(ids):
                total = jnp.zeros((len(ids), 2, seg, key_rows.shape[3]), jnp.float32)
                for offset, dk_term, dv_term in key_terms[m]:
                    hit = (jnp.array(ids, jnp.int32) == offset)[:, None, None, None]
                    total = total + jnp.where(hit, jnp.stack([dk_term, dv_term])[None], 0.0)
                return total

            keep = spread(range(0, node_count, 2))
            send = spread(range(1, node_count, 2)).astype(jnp.bfloat16)
            for bit in range(bits):
                held = keep + swap(send, bit).astype(jnp.float32)
                if bit + 1 < bits:
                    keep = held[0::2]
                    send = held[1::2].astype(jnp.bfloat16)
            received[m] = held[0]
    key_grad = jnp.stack(key_grads)[:, None]
    value_grad = jnp.stack(value_grads)[:, None]
    return query_grad, key_grad, value_grad


def solution(mesh):
    wide = P(None, "branch", None, "head")
    in_specs = (wide, wide, wide, wide, P("head", None), P(), P())
    return jax.shard_map(
        functools.partial(local, mesh.shape["branch"], mesh.shape["head"]),
        mesh=mesh,
        in_specs=in_specs,
        out_specs=(wide, wide, wide),
        check_vma=False,
    )
```

```python
import functools

import jax
import jax.numpy as jnp
from jax import lax
from jax.experimental import pallas as pl
from jax.experimental.pallas import tpu as pltpu
from jax.sharding import PartitionSpec as P

HD = 128
MASKED = -1e30
NT = (((1,), (1,)), ((), ()))
NN = (((1,), (0,)), ((), ()))
TN = (((0,), (0,)), ((), ()))


def pick_row(table, index_value):
    return lax.dynamic_index_in_dim(table, index_value, 0, keepdims=False)


def attention_kernel(level, fused, has_base, info_ref, q_ref, cot_ref, *refs):
    blocks = level + 1
    if fused:
        weight_ref, refs = refs[0], refs[1:]
    key_refs, value_refs = refs[:blocks], refs[blocks : 2 * blocks]
    dq_ref, dk_ref, dv_ref = refs[2 * blocks + has_base :]
    seg = cot_ref.shape[0]
    heads = q_ref.shape[3] // HD
    scale = 1.0 / HD**0.5
    own_len = info_ref[4 + level]
    keys = [ref[...].reshape(seg, HD) for ref in key_refs]
    values = [ref[...].reshape(seg, HD) for ref in value_refs]
    key_pos = lax.broadcasted_iota(jnp.int32, (seg, seg), 0)
    query_pos = lax.broadcasted_iota(jnp.int32, (seg, seg), 1)

    def dot(a, b, dims):
        return lax.dot_general(a, b, dims, preferred_element_type=jnp.float32)

    @pl.when(pl.program_id(1) == 0)
    def _():
        dk_ref[...] = jnp.zeros_like(dk_ref)
        dv_ref[...] = jnp.zeros_like(dv_ref)

    if fused:
        douts = dot(cot_ref[...], weight_ref[...], NT).astype(jnp.bfloat16)
    else:
        douts = cot_ref[...]
    row = lax.broadcasted_iota(jnp.int32, douts.shape, 0)
    douts = jnp.where(row < own_len, douts, jnp.zeros_like(douts))
    for h in range(heads):
        columns = slice(h * HD, (h + 1) * HD)
        q = q_ref[0, 0, :, columns]
        dout = douts[:, columns]
        scores = []
        for m in range(blocks):
            allowed = key_pos < info_ref[4 + m]
            if m == level:
                allowed = allowed & (key_pos <= query_pos)
            scores.append(jnp.where(allowed, dot(keys[m], q, NT), MASKED))
        top = functools.reduce(jnp.maximum, [jnp.max(s, axis=0, keepdims=True) for s in scores])
        exps = [jnp.exp((s - top) * scale) for s in scores]
        total = functools.reduce(jnp.add, [jnp.sum(e, axis=0, keepdims=True) for e in exps])
        inverse = 1.0 / total
        probs = [e * inverse for e in exps]
        narrow = [p.astype(jnp.bfloat16) for p in probs]
        dprobs = [dot(v, dout, NT) for v in values]
        delta = functools.reduce(
            jnp.add,
            [
                jnp.sum(pb.astype(jnp.float32) * dp, axis=0, keepdims=True)
                for pb, dp in zip(narrow, dprobs)
            ],
        )
        dq = jnp.zeros((HD, seg), jnp.float32)
        for m in range(blocks):
            ds = (probs[m] * (dprobs[m] - delta)).astype(jnp.bfloat16)
            dk_ref[m] += dot(ds, q, NN) * scale
            dv_ref[m] += dot(narrow[m], dout, NN)
            dq = dq + dot(keys[m], ds, TN)
        dq_ref[0, 0, :, columns] = (dq * scale).T.astype(jnp.bfloat16)


def attention_level(level, row_block, info, queries, cot, weight, key_rows, value_rows, kv_all, base):
    levels, _, seg, q_width = queries.shape
    kv_width = key_rows.shape[3]
    kv_local = kv_width // HD
    group = q_width // kv_width
    blocks = level + 1
    heads = min(4, group)
    steps = group // heads
    fused = weight is not None

    def gathered(kind, m):
        return pl.BlockSpec(
            (1, 1, 1, seg, HD), lambda n, g, info, m=m, k=kind: (info[m], m, k, 0, n)
        )

    q_spec = pl.BlockSpec(
        (1, 1, seg, heads * HD), lambda n, g, info: (level, 0, 0, n * steps + g)
    )
    own_spec = pl.BlockSpec((1, 1, seg, HD), lambda n, g, info: (level, 0, 0, n))
    if fused:
        model = weight.shape[1]
        products_in = 2 * seg * model * q_width
        cot_specs = [
            pl.BlockSpec((seg, model), lambda n, g, info: (row_block, 0)),
            pl.BlockSpec((heads * HD, model), lambda n, g, info: (n * steps + g, 0)),
        ]
        cots = [cot, weight]
    else:
        products_in = 0
        cot_specs = [
            pl.BlockSpec((seg, heads * HD), lambda n, g, info: (row_block, n * steps + g))
        ]
        cots = [cot]
    grad_spec = pl.BlockSpec((blocks, seg, HD), lambda n, g, info: (0, 0, n))
    in_specs = [q_spec] + cot_specs
    in_specs += [gathered(0, m) for m in range(level)] + [own_spec]
    in_specs += [gathered(1, m) for m in range(level)] + [own_spec]
    operands = [queries] + cots
    operands += [kv_all] * level + [key_rows] + [kv_all] * level + [value_rows]
    aliases = {}
    if base is not None:
        in_specs.append(pl.BlockSpec(memory_space=pl.ANY))
        operands.append(base)
        aliases = {len(operands): 0}
    grad_shape = jax.ShapeDtypeStruct((blocks, seg, kv_width), jnp.float32)
    products = 5 * 2 * seg * seg * HD * blocks * kv_local * group
    return pl.pallas_call(
        functools.partial(attention_kernel, level, fused, int(base is not None)),
        grid_spec=pltpu.PrefetchScalarGridSpec(
            num_scalar_prefetch=1,
            grid=(kv_local, steps),
            in_specs=in_specs,
            out_specs=[q_spec, grad_spec, grad_spec],
        ),
        out_shape=[jax.ShapeDtypeStruct(queries.shape, jnp.bfloat16), grad_shape, grad_shape],
        input_output_aliases=aliases,
        compiler_params=pltpu.CompilerParams(vmem_limit_bytes=52 * 1024 * 1024),
        cost_estimate=pl.CostEstimate(
            flops=4 * products + products_in,
            bytes_accessed=3 * seg * q_width * 2,
            transcendentals=seg * seg * blocks * kv_local * group,
        ),
        name="attention_level",
    )(info, *operands)


def local(node_count, queries, key_rows, value_rows, cotangent, out_weight, parents, seg_len):
    levels, _, seg, q_width = queries.shape
    bits = node_count.bit_length() - 1
    me = lax.axis_index("branch")

    def swap(array, bit):
        pairs = [(i, i ^ (1 << bit)) for i in range(node_count)]
        return lax.ppermute(array, "branch", pairs)

    width = cotangent.shape[3]
    gathered = {}

    def gather(first, last, rows):
        rows = rows.reshape((last - first) * seg, width)
        gathered[first] = lax.all_gather(rows, "head", axis=1, tiled=True)

    gather(levels - 2, levels, cotangent[levels - 2 :, 0])
    kv_all = jnp.stack([key_rows[: levels - 1, 0], value_rows[: levels - 1, 0]], axis=1)[None]
    waiting = list(range(levels - 2))
    for bit in reversed(range(bits)):
        arrived = swap(kv_all, bit)
        if bit < len(waiting):
            level = waiting.pop()
            rows, arrived = lax.optimization_barrier((cotangent[level, 0], arrived))
            gather(level, level + 1, rows)
        kv_all = jnp.concatenate([kv_all, arrived], axis=0)

    offsets = []
    infos = []
    for level in range(levels):
        lineage = [None] * (level + 1)
        lineage[level] = me
        for m in reversed(range(level)):
            lineage[m] = pick_row(parents[m], lineage[m + 1])
        relative = [node ^ me for node in lineage]
        slots = [
            sum(((r >> b) & 1) << (bits - 1 - b) for b in range(bits)) for r in relative
        ]
        lengths = [pick_row(seg_len[m], lineage[m]) for m in range(level + 1)]
        pad = [jnp.int32(0)] * (levels - 1 - level)
        infos.append(jnp.stack(slots + pad + lengths + pad).astype(jnp.int32))
        offsets.append(relative)

    key_terms = [[] for _ in range(levels)]
    received = [None] * (levels - 1)
    key_grads = [None] * levels
    value_grads = [None] * levels
    query_grad = None
    for level in reversed(range(levels)):
        first = min(level, levels - 2)
        if level == 0:
            gathered[0], *received = lax.optimization_barrier((gathered[0], *received))
        if level == 0:
            cot, weight = gathered[0], out_weight
        else:
            if level == levels - 1 or level < levels - 2:
                dout = lax.dot_general(
                    gathered[first], out_weight, NT, preferred_element_type=jnp.float32
                ).astype(jnp.bfloat16)
            cot, weight = dout, None
        query_grad, dk, dv = attention_level(
            level, level - first, infos[level], queries, cot, weight,
            key_rows, value_rows, kv_all, query_grad,
        )
        own = jnp.stack([dk[level], dv[level]])
        if level < levels - 1:
            own = own + received[level]
        key_grads[level] = own[0].astype(jnp.bfloat16)
        value_grads[level] = own[1].astype(jnp.bfloat16)
        for m in range(level):
            key_terms[m].append((offsets[level][m], dk[m], dv[m]))
        if level > 0:
            m = level - 1

            def spread(ids):
                total = jnp.zeros((len(ids), 2, seg, key_rows.shape[3]), jnp.float32)
                for offset, dk_term, dv_term in key_terms[m]:
                    hit = (jnp.array(ids, jnp.int32) == offset)[:, None, None, None]
                    total = total + jnp.where(hit, jnp.stack([dk_term, dv_term])[None], 0.0)
                return total

            keep = spread(range(0, node_count, 2))
            send = spread(range(1, node_count, 2)).astype(jnp.bfloat16)
            for bit in range(bits):
                held = keep + swap(send, bit).astype(jnp.float32)
                if bit + 1 < bits:
                    keep = held[0::2]
                    send = held[1::2].astype(jnp.bfloat16)
            received[m] = held[0]
    key_grad = jnp.stack(key_grads)[:, None]
    value_grad = jnp.stack(value_grads)[:, None]
    return query_grad, key_grad, value_grad


def solution(mesh):
    wide = P(None, "branch", None, "head")
    in_specs = (wide, wide, wide, wide, P("head", None), P(), P())
    return jax.shard_map(
        functools.partial(local, mesh.shape["branch"]),
        mesh=mesh,
        in_specs=in_specs,
        out_specs=(wide, wide, wide),
        check_vma=False,
    )
```

```python
import functools

import jax
import jax.numpy as jnp
from jax import lax
from jax.experimental import pallas as pl
from jax.experimental.pallas import tpu as pltpu
from jax.sharding import PartitionSpec as P

HD = 128
MASKED = -1e30
NT = (((1,), (1,)), ((), ()))
NN = (((1,), (0,)), ((), ()))
TN = (((0,), (0,)), ((), ()))


def pick_row(table, index_value):
    return lax.dynamic_index_in_dim(table, index_value, 0, keepdims=False)


def attention_kernel(level, fused, has_base, info_ref, q_ref, cot_ref, *refs):
    blocks = level + 1
    if fused:
        weight_ref, refs = refs[0], refs[1:]
    key_refs, value_refs = refs[:blocks], refs[blocks : 2 * blocks]
    dq_ref, dk_ref, dv_ref = refs[2 * blocks + has_base :]
    seg = cot_ref.shape[0]
    heads = q_ref.shape[3] // HD
    scale = 1.0 / HD**0.5
    own_len = info_ref[4 + level]
    keys = [ref[...].reshape(seg, HD) for ref in key_refs]
    values = [ref[...].reshape(seg, HD) for ref in value_refs]
    key_pos = lax.broadcasted_iota(jnp.int32, (seg, seg), 0)
    query_pos = lax.broadcasted_iota(jnp.int32, (seg, seg), 1)

    def dot(a, b, dims):
        return lax.dot_general(a, b, dims, preferred_element_type=jnp.float32)

    @pl.when(pl.program_id(1) == 0)
    def _():
        dk_ref[...] = jnp.zeros_like(dk_ref)
        dv_ref[...] = jnp.zeros_like(dv_ref)

    if fused:
        douts = dot(cot_ref[...], weight_ref[...], NT).astype(jnp.bfloat16)
    else:
        douts = cot_ref[...]
    row = lax.broadcasted_iota(jnp.int32, douts.shape, 0)
    douts = jnp.where(row < own_len, douts, jnp.zeros_like(douts))
    for h in range(heads):
        columns = slice(h * HD, (h + 1) * HD)
        q = q_ref[0, 0, :, columns]
        dout = douts[:, columns]
        scores = []
        for m in range(blocks):
            allowed = key_pos < info_ref[4 + m]
            if m == level:
                allowed = allowed & (key_pos <= query_pos)
            scores.append(jnp.where(allowed, dot(keys[m], q, NT), MASKED))
        top = functools.reduce(jnp.maximum, [jnp.max(s, axis=0, keepdims=True) for s in scores])
        exps = [jnp.exp((s - top) * scale) for s in scores]
        total = functools.reduce(jnp.add, [jnp.sum(e, axis=0, keepdims=True) for e in exps])
        inverse = 1.0 / total
        probs = [e * inverse for e in exps]
        narrow = [p.astype(jnp.bfloat16) for p in probs]
        dprobs = [dot(v, dout, NT) for v in values]
        delta = functools.reduce(
            jnp.add,
            [
                jnp.sum(pb.astype(jnp.float32) * dp, axis=0, keepdims=True)
                for pb, dp in zip(narrow, dprobs)
            ],
        )
        dq = jnp.zeros((HD, seg), jnp.float32)
        for m in range(blocks):
            ds = (probs[m] * (dprobs[m] - delta)).astype(jnp.bfloat16)
            dk_ref[m] += dot(ds, q, NN) * scale
            dv_ref[m] += dot(narrow[m], dout, NN)
            dq = dq + dot(keys[m], ds, TN)
        dq_ref[0, 0, :, columns] = (dq * scale).T.astype(jnp.bfloat16)


def attention_level(level, row_block, info, queries, cot, weight, key_rows, value_rows, kv_all, base):
    levels, _, seg, q_width = queries.shape
    kv_width = key_rows.shape[3]
    kv_local = kv_width // HD
    group = q_width // kv_width
    blocks = level + 1
    heads = min(4, group)
    steps = group // heads
    fused = weight is not None

    def gathered(kind, m):
        return pl.BlockSpec(
            (1, 1, 1, seg, HD), lambda n, g, info, m=m, k=kind: (info[m], m, k, 0, n)
        )

    q_spec = pl.BlockSpec(
        (1, 1, seg, heads * HD), lambda n, g, info: (level, 0, 0, n * steps + g)
    )
    own_spec = pl.BlockSpec((1, 1, seg, HD), lambda n, g, info: (level, 0, 0, n))
    if fused:
        model = weight.shape[1]
        products_in = 2 * seg * model * q_width
        cot_specs = [
            pl.BlockSpec((seg, model), lambda n, g, info: (row_block, 0)),
            pl.BlockSpec((heads * HD, model), lambda n, g, info: (n * steps + g, 0)),
        ]
        cots = [cot, weight]
    else:
        products_in = 0
        cot_specs = [
            pl.BlockSpec((seg, heads * HD), lambda n, g, info: (row_block, n * steps + g))
        ]
        cots = [cot]
    grad_spec = pl.BlockSpec((blocks, seg, HD), lambda n, g, info: (0, 0, n))
    in_specs = [q_spec] + cot_specs
    in_specs += [gathered(0, m) for m in range(level)] + [own_spec]
    in_specs += [gathered(1, m) for m in range(level)] + [own_spec]
    operands = [queries] + cots
    operands += [kv_all] * level + [key_rows] + [kv_all] * level + [value_rows]
    aliases = {}
    if base is not None:
        in_specs.append(pl.BlockSpec(memory_space=pl.ANY))
        operands.append(base)
        aliases = {len(operands): 0}
    grad_shape = jax.ShapeDtypeStruct((blocks, seg, kv_width), jnp.float32)
    products = 5 * 2 * seg * seg * HD * blocks * kv_local * group
    return pl.pallas_call(
        functools.partial(attention_kernel, level, fused, int(base is not None)),
        grid_spec=pltpu.PrefetchScalarGridSpec(
            num_scalar_prefetch=1,
            grid=(kv_local, steps),
            in_specs=in_specs,
            out_specs=[q_spec, grad_spec, grad_spec],
        ),
        out_shape=[jax.ShapeDtypeStruct(queries.shape, jnp.bfloat16), grad_shape, grad_shape],
        input_output_aliases=aliases,
        compiler_params=pltpu.CompilerParams(vmem_limit_bytes=52 * 1024 * 1024),
        cost_estimate=pl.CostEstimate(
            flops=4 * products + products_in,
            bytes_accessed=3 * seg * q_width * 2,
            transcendentals=seg * seg * blocks * kv_local * group,
        ),
        name="attention_level",
    )(info, *operands)


def local(node_count, queries, key_rows, value_rows, cotangent, out_weight, parents, seg_len):
    levels, _, seg, q_width = queries.shape
    bits = node_count.bit_length() - 1
    me = lax.axis_index("branch")

    def swap(array, bit):
        pairs = [(i, i ^ (1 << bit)) for i in range(node_count)]
        return lax.ppermute(array, "branch", pairs)

    width = cotangent.shape[3]
    chunks = [(levels - 2, levels)] + [(m, m + 1) for m in reversed(range(levels - 2))]
    gathered = {}
    for first, last in chunks:
        rows = cotangent[first:last, 0].reshape((last - first) * seg, width)
        gathered[first] = lax.all_gather(rows, "head", axis=1, tiled=True)

    kv_all = jnp.stack([key_rows[: levels - 1, 0], value_rows[: levels - 1, 0]], axis=1)[None]
    for bit in reversed(range(bits)):
        kv_all = jnp.concatenate([kv_all, swap(kv_all, bit)], axis=0)

    offsets = []
    infos = []
    for level in range(levels):
        lineage = [None] * (level + 1)
        lineage[level] = me
        for m in reversed(range(level)):
            lineage[m] = pick_row(parents[m], lineage[m + 1])
        relative = [node ^ me for node in lineage]
        slots = [
            sum(((r >> b) & 1) << (bits - 1 - b) for b in range(bits)) for r in relative
        ]
        lengths = [pick_row(seg_len[m], lineage[m]) for m in range(level + 1)]
        pad = [jnp.int32(0)] * (levels - 1 - level)
        infos.append(jnp.stack(slots + pad + lengths + pad).astype(jnp.int32))
        offsets.append(relative)

    key_terms = [[] for _ in range(levels)]
    received = [None] * (levels - 1)
    key_grads = [None] * levels
    value_grads = [None] * levels
    query_grad = None
    for level in reversed(range(levels)):
        first = min(level, levels - 2)
        if level == 0:
            gathered[0], *received = lax.optimization_barrier((gathered[0], *received))
        elif level < levels - 2:
            gathered[level], dk = lax.optimization_barrier((gathered[level], dk))
        if level == 0:
            cot, weight = gathered[0], out_weight
        else:
            if level == levels - 1 or level < levels - 2:
                dout = lax.dot_general(
                    gathered[first], out_weight, NT, preferred_element_type=jnp.float32
                ).astype(jnp.bfloat16)
            cot, weight = dout, None
        query_grad, dk, dv = attention_level(
            level, level - first, infos[level], queries, cot, weight,
            key_rows, value_rows, kv_all, query_grad,
        )
        own = jnp.stack([dk[level], dv[level]])
        if level < levels - 1:
            own = own + received[level]
        key_grads[level] = own[0].astype(jnp.bfloat16)
        value_grads[level] = own[1].astype(jnp.bfloat16)
        for m in range(level):
            key_terms[m].append((offsets[level][m], dk[m], dv[m]))
        if level > 0:
            m = level - 1

            def spread(ids):
                total = jnp.zeros((len(ids), 2, seg, key_rows.shape[3]), jnp.float32)
                for offset, dk_term, dv_term in key_terms[m]:
                    hit = (jnp.array(ids, jnp.int32) == offset)[:, None, None, None]
                    total = total + jnp.where(hit, jnp.stack([dk_term, dv_term])[None], 0.0)
                return total

            keep = spread(range(0, node_count, 2))
            send = spread(range(1, node_count, 2)).astype(jnp.bfloat16)
            for bit in range(bits):
                held = keep + swap(send, bit).astype(jnp.float32)
                if bit + 1 < bits:
                    keep = held[0::2]
                    send = held[1::2].astype(jnp.bfloat16)
            received[m] = held[0]
    key_grad = jnp.stack(key_grads)[:, None]
    value_grad = jnp.stack(value_grads)[:, None]
    return query_grad, key_grad, value_grad


def solution(mesh):
    wide = P(None, "branch", None, "head")
    in_specs = (wide, wide, wide, wide, P("head", None), P(), P())
    return jax.shard_map(
        functools.partial(local, mesh.shape["branch"]),
        mesh=mesh,
        in_specs=in_specs,
        out_specs=(wide, wide, wide),
        check_vma=False,
    )
```

```python
import functools

import jax
import jax.numpy as jnp
from jax import lax
from jax.experimental import pallas as pl
from jax.experimental.pallas import tpu as pltpu
from jax.sharding import PartitionSpec as P

HD = 128
MASKED = -1e30
NT = (((1,), (1,)), ((), ()))
NN = (((1,), (0,)), ((), ()))
TN = (((0,), (0,)), ((), ()))


def pick_row(table, index_value):
    return lax.dynamic_index_in_dim(table, index_value, 0, keepdims=False)


def attention_kernel(level, fused, has_base, info_ref, q_ref, cot_ref, *refs):
    blocks = level + 1
    if fused:
        weight_ref, probs_ref, refs = refs[0], refs[1], refs[2:]
    key_refs, value_refs = refs[:blocks], refs[blocks : 2 * blocks]
    dq_ref, dk_ref, dv_ref = refs[2 * blocks + has_base :]
    seg = cot_ref.shape[0]
    heads = q_ref.shape[3] // HD
    scale = 1.0 / HD**0.5
    own_len = info_ref[4 + level]
    keys = [ref[...].reshape(seg, HD) for ref in key_refs]
    values = [ref[...].reshape(seg, HD) for ref in value_refs]
    key_pos = lax.broadcasted_iota(jnp.int32, (seg, seg), 0)
    query_pos = lax.broadcasted_iota(jnp.int32, (seg, seg), 1)

    def dot(a, b, dims):
        return lax.dot_general(a, b, dims, preferred_element_type=jnp.float32)

    @pl.when(pl.program_id(1) == 0)
    def _():
        dk_ref[...] = jnp.zeros_like(dk_ref)
        dv_ref[...] = jnp.zeros_like(dv_ref)

    if fused:
        douts = dot(cot_ref[...], weight_ref[...], NT).astype(jnp.bfloat16)
    else:
        douts = cot_ref[...]
    row = lax.broadcasted_iota(jnp.int32, douts.shape, 0)
    douts = jnp.where(row < own_len, douts, jnp.zeros_like(douts))
    for h in range(heads):
        columns = slice(h * HD, (h + 1) * HD)
        q = q_ref[0, 0, :, columns]
        dout = douts[:, columns]
        if fused:
            probs = [probs_ref[h]]
        else:
            scores = []
            for m in range(blocks):
                allowed = key_pos < info_ref[4 + m]
                if m == level:
                    allowed = allowed & (key_pos <= query_pos)
                scores.append(jnp.where(allowed, dot(keys[m], q, NT), MASKED))
            top = functools.reduce(jnp.maximum, [jnp.max(s, axis=0, keepdims=True) for s in scores])
            exps = [jnp.exp((s - top) * scale) for s in scores]
            total = functools.reduce(jnp.add, [jnp.sum(e, axis=0, keepdims=True) for e in exps])
            inverse = 1.0 / total
            probs = [e * inverse for e in exps]
        narrow = [p.astype(jnp.bfloat16) for p in probs]
        dprobs = [dot(v, dout, NT) for v in values]
        delta = functools.reduce(
            jnp.add,
            [
                jnp.sum(pb.astype(jnp.float32) * dp, axis=0, keepdims=True)
                for pb, dp in zip(narrow, dprobs)
            ],
        )
        dq = jnp.zeros((HD, seg), jnp.float32)
        for m in range(blocks):
            ds = (probs[m] * (dprobs[m] - delta)).astype(jnp.bfloat16)
            dk_ref[m] += dot(ds, q, NN) * scale
            dv_ref[m] += dot(narrow[m], dout, NN)
            dq = dq + dot(keys[m], ds, TN)
        dq_ref[0, 0, :, columns] = (dq * scale).T.astype(jnp.bfloat16)


def probs_kernel(info_ref, q_ref, key_ref, probs_ref):
    seg = q_ref.shape[2]
    scale = 1.0 / HD**0.5
    key_pos = lax.broadcasted_iota(jnp.int32, (seg, seg), 0)
    query_pos = lax.broadcasted_iota(jnp.int32, (seg, seg), 1)
    allowed = (key_pos < info_ref[4]) & (key_pos <= query_pos)
    for h in range(probs_ref.shape[0]):
        q = q_ref[0, 0, :, h * HD : (h + 1) * HD]
        score = lax.dot_general(key_ref[0, 0], q, NT, preferred_element_type=jnp.float32)
        score = jnp.where(allowed, score, MASKED)
        e = jnp.exp((score - jnp.max(score, axis=0, keepdims=True)) * scale)
        probs_ref[h] = e * (1.0 / jnp.sum(e, axis=0, keepdims=True))


def first_probs(info, queries, key_rows):
    seg, q_width, kv_width = queries.shape[2], queries.shape[3], key_rows.shape[3]
    kv_local, group = kv_width // HD, q_width // kv_width
    heads = min(4, group)
    steps = group // heads
    return pl.pallas_call(
        probs_kernel,
        grid_spec=pltpu.PrefetchScalarGridSpec(
            num_scalar_prefetch=1,
            grid=(kv_local, steps),
            in_specs=[
                pl.BlockSpec((1, 1, seg, heads * HD), lambda n, g, info: (0, 0, 0, n * steps + g)),
                pl.BlockSpec((1, 1, seg, HD), lambda n, g, info: (0, 0, 0, n)),
            ],
            out_specs=pl.BlockSpec((heads, seg, seg), lambda n, g, info: (n * steps + g, 0, 0)),
        ),
        out_shape=jax.ShapeDtypeStruct((kv_local * group, seg, seg), jnp.float32),
        compiler_params=pltpu.CompilerParams(vmem_limit_bytes=32 * 1024 * 1024),
        name="first_probs",
    )(info, queries, key_rows)


def attention_level(level, row_block, info, queries, cot, weight, key_rows, value_rows, kv_all, base, probs):
    levels, _, seg, q_width = queries.shape
    kv_width = key_rows.shape[3]
    kv_local = kv_width // HD
    group = q_width // kv_width
    blocks = level + 1
    heads = min(4, group)
    steps = group // heads
    fused = weight is not None

    def gathered(kind, m):
        return pl.BlockSpec(
            (1, 1, 1, seg, HD), lambda n, g, info, m=m, k=kind: (info[m], m, k, 0, n)
        )

    q_spec = pl.BlockSpec(
        (1, 1, seg, heads * HD), lambda n, g, info: (level, 0, 0, n * steps + g)
    )
    own_spec = pl.BlockSpec((1, 1, seg, HD), lambda n, g, info: (level, 0, 0, n))
    if fused:
        model = weight.shape[1]
        products_in = 2 * seg * model * q_width
        cot_specs = [
            pl.BlockSpec((seg, model), lambda n, g, info: (row_block, 0)),
            pl.BlockSpec((heads * HD, model), lambda n, g, info: (n * steps + g, 0)),
            pl.BlockSpec((heads, seg, seg), lambda n, g, info: (n * steps + g, 0, 0)),
        ]
        cots = [cot, weight, probs]
    else:
        products_in = 0
        cot_specs = [
            pl.BlockSpec((seg, heads * HD), lambda n, g, info: (row_block, n * steps + g))
        ]
        cots = [cot]
    grad_spec = pl.BlockSpec((blocks, seg, HD), lambda n, g, info: (0, 0, n))
    in_specs = [q_spec] + cot_specs
    in_specs += [gathered(0, m) for m in range(level)] + [own_spec]
    in_specs += [gathered(1, m) for m in range(level)] + [own_spec]
    operands = [queries] + cots
    operands += [kv_all] * level + [key_rows] + [kv_all] * level + [value_rows]
    aliases = {}
    if base is not None:
        in_specs.append(pl.BlockSpec(memory_space=pl.ANY))
        operands.append(base)
        aliases = {len(operands): 0}
    grad_shape = jax.ShapeDtypeStruct((blocks, seg, kv_width), jnp.float32)
    products = 5 * 2 * seg * seg * HD * blocks * kv_local * group
    return pl.pallas_call(
        functools.partial(attention_kernel, level, fused, int(base is not None)),
        grid_spec=pltpu.PrefetchScalarGridSpec(
            num_scalar_prefetch=1,
            grid=(kv_local, steps),
            in_specs=in_specs,
            out_specs=[q_spec, grad_spec, grad_spec],
        ),
        out_shape=[jax.ShapeDtypeStruct(queries.shape, jnp.bfloat16), grad_shape, grad_shape],
        input_output_aliases=aliases,
        compiler_params=pltpu.CompilerParams(vmem_limit_bytes=52 * 1024 * 1024),
        cost_estimate=pl.CostEstimate(
            flops=4 * products + products_in,
            bytes_accessed=3 * seg * q_width * 2,
            transcendentals=seg * seg * blocks * kv_local * group,
        ),
        name="attention_level",
    )(info, *operands)


def local(node_count, queries, key_rows, value_rows, cotangent, out_weight, parents, seg_len):
    levels, _, seg, q_width = queries.shape
    bits = node_count.bit_length() - 1
    me = lax.axis_index("branch")

    def swap(array, bit):
        pairs = [(i, i ^ (1 << bit)) for i in range(node_count)]
        return lax.ppermute(array, "branch", pairs)

    width = cotangent.shape[3]
    chunks = [(levels - 2, levels)] + [(m, m + 1) for m in reversed(range(levels - 2))]
    gathered = {}
    for first, last in chunks:
        rows = cotangent[first:last, 0].reshape((last - first) * seg, width)
        gathered[first] = lax.all_gather(rows, "head", axis=1, tiled=True)

    kv_all = jnp.stack([key_rows[: levels - 1, 0], value_rows[: levels - 1, 0]], axis=1)[None]
    for bit in reversed(range(bits)):
        kv_all = jnp.concatenate([kv_all, swap(kv_all, bit)], axis=0)

    offsets = []
    infos = []
    for level in range(levels):
        lineage = [None] * (level + 1)
        lineage[level] = me
        for m in reversed(range(level)):
            lineage[m] = pick_row(parents[m], lineage[m + 1])
        relative = [node ^ me for node in lineage]
        slots = [
            sum(((r >> b) & 1) << (bits - 1 - b) for b in range(bits)) for r in relative
        ]
        lengths = [pick_row(seg_len[m], lineage[m]) for m in range(level + 1)]
        pad = [jnp.int32(0)] * (levels - 1 - level)
        infos.append(jnp.stack(slots + pad + lengths + pad).astype(jnp.int32))
        offsets.append(relative)

    key_terms = [[] for _ in range(levels)]
    received = [None] * (levels - 1)
    key_grads = [None] * levels
    value_grads = [None] * levels
    query_grad = None
    probs = first_probs(infos[0], queries, key_rows)
    for level in reversed(range(levels)):
        first = min(level, levels - 2)
        if level == 0:
            gathered[0], *received = lax.optimization_barrier((gathered[0], *received))
        elif level < levels - 2:
            gathered[level], dk, probs = lax.optimization_barrier((gathered[level], dk, probs))
        if level == 0:
            cot, weight = gathered[0], out_weight
        else:
            if level == levels - 1 or level < levels - 2:
                dout = lax.dot_general(
                    gathered[first], out_weight, NT, preferred_element_type=jnp.float32
                ).astype(jnp.bfloat16)
            cot, weight = dout, None
        query_grad, dk, dv = attention_level(
            level, level - first, infos[level], queries, cot, weight,
            key_rows, value_rows, kv_all, query_grad, probs,
        )
        own = jnp.stack([dk[level], dv[level]])
        if level < levels - 1:
            own = own + received[level]
        key_grads[level] = own[0].astype(jnp.bfloat16)
        value_grads[level] = own[1].astype(jnp.bfloat16)
        for m in range(level):
            key_terms[m].append((offsets[level][m], dk[m], dv[m]))
        if level > 0:
            m = level - 1

            def spread(ids):
                total = jnp.zeros((len(ids), 2, seg, key_rows.shape[3]), jnp.float32)
                for offset, dk_term, dv_term in key_terms[m]:
                    hit = (jnp.array(ids, jnp.int32) == offset)[:, None, None, None]
                    total = total + jnp.where(hit, jnp.stack([dk_term, dv_term])[None], 0.0)
                return total

            keep = spread(range(0, node_count, 2))
            send = spread(range(1, node_count, 2)).astype(jnp.bfloat16)
            for bit in range(bits):
                held = keep + swap(send, bit).astype(jnp.float32)
                if bit + 1 < bits:
                    keep = held[0::2]
                    send = held[1::2].astype(jnp.bfloat16)
            received[m] = held[0]
    key_grad = jnp.stack(key_grads)[:, None]
    value_grad = jnp.stack(value_grads)[:, None]
    return query_grad, key_grad, value_grad


def solution(mesh):
    wide = P(None, "branch", None, "head")
    in_specs = (wide, wide, wide, wide, P("head", None), P(), P())
    return jax.shard_map(
        functools.partial(local, mesh.shape["branch"]),
        mesh=mesh,
        in_specs=in_specs,
        out_specs=(wide, wide, wide),
        check_vma=False,
    )
```
